32 devices in a mesh: depth: 4 (over y, core), row: 2 (over x), col: 4 (over z).
Axes of the slice: x: 2, y: 2, z: 4, core: 2. Of those that a mesh axis runs over, the one named last changes fastest.
Arguments:
- expression: bfloat16 [3072, 8192], P('depth', 'col'), as said below
- offsets: int32 [4], P('depth'), may hold values from 0 to 256
Outputs:
- margin: float32 [8192, 8192], P('row', 'col')
The draws below stay inside these ranges and needn't reach their ends.
Inputs may be any that keep to these rules, and one draw needn't show every extreme that they name: `expression`: finite values.
All inputs are finite; a program needn't handle non-finite values.
Results may differ from the reference program's by a relative error of at most 0.0003.
Values may be sent and summed in bfloat16 or wider, within the bound.
A program may use at most 256 MiB of HBM per device.

```python
import math
import jax
import jax.numpy as jnp
from jax import lax

G = 8192
CW_DEV = 512
MODULES = 64
POWER = 6
SLAB = 768
CELLS = 2048
ATLAS = 3072
N_DEPTH = 4


def draw_expression(key, part):
    key = jax.random.fold_in(key, 1)
    keys = jax.random.split(key, 10)
    broad_count = 4
    member_count = 3
    loads = jax.random.uniform(keys[1], (G,), jnp.float32, 0.55, 0.95)
    factors = jax.random.normal(keys[2], (ATLAS, MODULES), jnp.float32)
    broad = jax.random.normal(keys[6], (ATLAS, broad_count), jnp.float32)
    noise = jax.random.normal(keys[3], (ATLAS, G), jnp.float32)
    broad_weights = 0.8 * jax.random.normal(keys[7], (broad_count, G), jnp.float32)
    members = jax.random.randint(keys[0], (member_count, G), 0, MODULES)
    sizes = jax.random.uniform(keys[8], (member_count, G), jnp.float32, 0.5, 1.0)
    signs = jnp.where(jax.random.bernoulli(keys[9], 0.5, (member_count, G)), 1.0, -1.0)
    member_weights = sizes * signs
    signal = jnp.zeros((ATLAS, G), jnp.float32)
    for index in range(broad_count):
        signal = signal + broad[:, index:index + 1] * broad_weights[index][None, :]
    for index in range(member_count):
        signal = signal + jnp.take(factors, members[index], axis=1) * member_weights[index][None, :]
    strength = jnp.sqrt(jnp.sum(broad_weights * broad_weights, axis=0) + jnp.sum(member_weights * member_weights, axis=0))
    scale = jnp.exp(jax.random.uniform(keys[4], (G,), jnp.float32, math.log(0.3), math.log(3.0)))
    centre = jax.random.normal(keys[5], (G,), jnp.float32)
    values = centre + scale * (loads * signal / strength + jnp.sqrt(1.0 - loads * loads) * noise)
    return values.astype(jnp.bfloat16)


def with_ends(values, key, low, largest):
    index_at = [jax.random.randint(jax.random.fold_in(key, axis), (), 0, length) for axis, length in enumerate(values.shape)]
    longest = values.shape.index(max(values.shape))
    beside = index_at[:longest] + [(index_at[longest] + 1) % values.shape[longest]] + index_at[longest + 1:]
    return values.at[tuple(index_at)].set(low).at[tuple(beside)].set(largest)


def setup_inputs(seed: int = 0) -> dict:
    key_list = jax.random.split(jax.random.key(seed), 3)
    expression = draw_expression(jax.random.fold_in(key_list[2], 71), 0)
    offsets = with_ends(jax.random.randint(key_list[1], (N_DEPTH,), 0, SLAB - CW_DEV + 1), jax.random.fold_in(key_list[1], 1), 0, SLAB - CW_DEV).astype(jnp.int32)
    return {"expression": expression, "offsets": offsets}


def reference(expression, offsets):
    pieces = []
    for index in range(N_DEPTH):
        start = (index * SLAB + offsets[index]).astype(jnp.int32)
        pieces.append(lax.dynamic_slice_in_dim(expression, start, CW_DEV, 0))
    window = jnp.concatenate(pieces, axis=0)
    values = window.astype(jnp.float32)
    mean = lax.optimization_barrier(jnp.sum(values, axis=0)) / CELLS
    centred = values - mean
    variance = lax.optimization_barrier(jnp.sum(centred * centred, axis=0)) / CELLS
    scaled = (centred * lax.rsqrt(CELLS * (variance + 1e-05))).astype(jnp.bfloat16)
    wide = scaled.astype(jnp.float32)
    corr = jnp.dot(wide.T, wide, precision=lax.Precision.HIGHEST, preferred_element_type=jnp.float32)
    ident = jnp.arange(G)[:, None] == jnp.arange(G)[None, :]
    adjacency = jnp.where(ident, 0.0, lax.integer_pow(jnp.abs(corr), POWER))
    half = adjacency.astype(jnp.bfloat16).astype(jnp.float32)
    shared = jnp.dot(half, half, precision=lax.Precision.HIGHEST, preferred_element_type=jnp.float32)
    degree = lax.optimization_barrier(jnp.sum(adjacency, axis=1))
    denom = jnp.minimum(degree[:, None], degree[None, :]) + 1.0 - adjacency
    margin = (shared + adjacency) / denom
    return jnp.where(ident, 1.0, margin)
```

```python
import functools

import jax
import jax.numpy as jnp
from jax import lax
from jax.experimental import pallas as pl
from jax.experimental.pallas import tpu as pltpu
from jax.sharding import PartitionSpec as P

CW_DEV = 512
VMEM = 56 * 1024 * 1024
CHUNK = 256


def panel_kernel(rows_ref, x_ref, y_ref, *outs, n_cells, width, tiles):
    if tiles:
        half_ref, degree_ref, tile_ref = outs
    else:
        half_ref, degree_ref = outs
    i, j = pl.program_id(0), pl.program_id(1)
    block = half_ref.shape[0]
    shift = (j - (rows_ref[0] + i)) * block
    chunk = min(CHUNK, block)
    inside = (j >= rows_ref[1]) & (j < rows_ref[1] + width)
    partial = jnp.zeros((block, 128), jnp.float32)
    for start in range(0, block, chunk):
        corr = jnp.zeros((block, chunk), jnp.float32)
        for d in range(n_cells):
            corr = corr + lax.dot_general(
                x_ref[0, d, 0],
                y_ref[0, d, 0, start:start + chunk],
                (((1,), (1,)), ((), ())),
                preferred_element_type=jnp.float32,
            )
        square = corr * corr
        value = square * square * square
        gap = lax.broadcasted_iota(jnp.int32, value.shape, 0) - lax.broadcasted_iota(
            jnp.int32, value.shape, 1
        )
        value = jnp.where(gap == shift + start, 0.0, value)
        half_ref[:, start:start + chunk] = value.astype(jnp.bfloat16)
        for lane in range(0, chunk, 128):
            partial = partial + value[:, lane:lane + 128]
        if tiles:
            @pl.when(inside)
            def _(value=value, start=start):
                tile_ref[:, start:start + chunk] = value

    @pl.when(j == 0)
    def _():
        degree_ref[...] = partial

    @pl.when(j > 0)
    def _():
        degree_ref[...] += partial


def panel(cells, first, col_first, rows, width, block, genes, with_tile):
    n_row, n_cells, n_col, held, depth = cells.shape
    per_row = held // block
    per_col = per_row * n_row

    def place(g):
        rest = g % per_col
        return rest // per_row, 0, g // per_col, rest % per_row, 0

    n_i, n_j = rows // block, genes // block
    n_t = width // block
    shape = (1, n_cells, 1, block, depth)
    out_shape = [
        jax.ShapeDtypeStruct((rows, genes), jnp.bfloat16),
        jax.ShapeDtypeStruct((rows, 128), jnp.float32),
    ]
    out_specs = [
        pl.BlockSpec((block, block), lambda i, j, s: (i, j)),
        pl.BlockSpec((block, 128), lambda i, j, s: (i, 0)),
    ]
    if with_tile:
        out_shape.append(jax.ShapeDtypeStruct((rows, width), jnp.float32))
        out_specs.append(
            pl.BlockSpec(
                (block, block), lambda i, j, s: (i, jnp.clip(j - s[1], 0, n_t - 1))
            )
        )
    return pl.pallas_call(
        functools.partial(panel_kernel, n_cells=n_cells, width=n_t, tiles=with_tile),
        grid_spec=pltpu.PrefetchScalarGridSpec(
            num_scalar_prefetch=1,
            grid=(n_i, n_j),
            in_specs=[
                pl.BlockSpec(shape, lambda i, j, s: place(s[0] + i)),
                pl.BlockSpec(shape, lambda i, j, s: place(j)),
            ],
            out_specs=out_specs,
        ),
        out_shape=out_shape,
        compiler_params=pltpu.CompilerParams(vmem_limit_bytes=VMEM),
        cost_estimate=pl.CostEstimate(
            flops=2 * rows * genes * n_cells * depth,
            bytes_accessed=rows * genes * 2 + 2 * genes * n_cells * depth * n_i,
            transcendentals=0,
        ),
        name="adjacency_tiled" if with_tile else "adjacency",
    )(jnp.stack([first, col_first]).astype(jnp.int32), cells, cells)


def margin_kernel(s_ref, a_ref, b_ref, tile_ref, kr_ref, kc_ref, *rest):
    piece_ref, full_ref, total = rest[-3:]
    i, k = pl.program_id(0), pl.program_id(1)
    last = pl.num_programs(1) - 1
    rows, cols = piece_ref.shape
    part = lax.dot_general(
        a_ref[...], b_ref[...], (((1,), (1,)), ((), ())), preferred_element_type=jnp.float32
    )

    @pl.when(k == 0)
    def _():
        total[...] = part

    @pl.when((k > 0) & (k < last))
    def _():
        total[...] += part

    @pl.when(k == last)
    def _():
        adj = tile_ref[...]
        shared = total[...] + part
        denom = jnp.minimum(kr_ref[...], kc_ref[...]) + 1.0 - adj
        result = (shared + adj) / denom
        gap = lax.broadcasted_iota(jnp.int32, (rows, cols), 0) - lax.broadcasted_iota(
            jnp.int32, (rows, cols), 1
        )
        result = jnp.where(gap == s_ref[1] - i * rows, 1.0, result)
        piece_ref[...] = result
        full_ref[...] = result


def margin_piece(left, right, tile, k_rows, k_cols, index, pieces, core, gap, whole):
    rows, genes = left.shape
    cols = right.shape[0]
    size = rows // pieces
    step = min(1024, genes)
    in_specs = [
        pl.BlockSpec((size, step), lambda i, k, s: (index, k)),
        pl.BlockSpec((cols, step), lambda i, k, s: (0, k)),
        pl.BlockSpec((size, cols), lambda i, k, s: (index, 0)),
        pl.BlockSpec((size, 1), lambda i, k, s: (index, 0)),
        pl.BlockSpec((1, cols), lambda i, k, s: (0, 0)),
    ]
    args = [left, right, tile, k_rows, k_cols]
    aliases = {}
    if whole is not None:
        in_specs.append(pl.BlockSpec(memory_space=pl.ANY))
        args.append(whole)
        aliases = {6: 1}
    return pl.pallas_call(
        margin_kernel,
        grid_spec=pltpu.PrefetchScalarGridSpec(
            num_scalar_prefetch=1,
            grid=(1, genes // step),
            in_specs=in_specs,
            out_specs=[
                pl.BlockSpec((size, cols), lambda i, k, s: (0, 0)),
                pl.BlockSpec((size, cols), lambda i, k, s: (s[0], 0)),
            ],
            scratch_shapes=[pltpu.VMEM((size, cols), jnp.float32)],
        ),
        out_shape=[
            jax.ShapeDtypeStruct((size, cols), jnp.float32),
            jax.ShapeDtypeStruct((2 * rows, cols), jnp.float32),
        ],
        input_output_aliases=aliases,
        compiler_params=pltpu.CompilerParams(vmem_limit_bytes=VMEM),
        cost_estimate=pl.CostEstimate(
            flops=2 * size * genes * cols,
            bytes_accessed=2 * (size + cols) * genes + 12 * size * cols,
            transcendentals=0,
        ),
        name="margin",
    )(jnp.stack([core * pieces + index, gap - index * size]).astype(jnp.int32), *args)


def on_device(expression, offsets):
    n_row = lax.axis_size("row")
    n_col = lax.axis_size("col")
    n_depth = lax.axis_size("depth")
    row_id, col_id = lax.axis_index("row"), lax.axis_index("col")
    core = lax.axis_index("depth") % 2
    tile_cols = expression.shape[1]
    genes = tile_cols * n_col
    tile_rows = genes // n_row
    rows = tile_rows // 2
    cells_all = CW_DEV * n_depth
    window = lax.dynamic_slice_in_dim(expression, offsets[0], CW_DEV, 0)
    values = window.astype(jnp.float32)
    mean = lax.psum(jnp.sum(values, axis=0), "depth") / cells_all
    centred = values - mean
    variance = lax.psum(jnp.sum(centred * centred, axis=0), "depth") / cells_all
    held = tile_cols // n_row
    scale = lax.rsqrt(cells_all * (variance + 1e-05))
    mine = lax.dynamic_slice_in_dim(centred, row_id * held, held, 1)
    scale = lax.dynamic_slice_in_dim(scale, row_id * held, held, 0)
    scaled = (mine * scale).astype(jnp.bfloat16).T
    cells = lax.all_gather(scaled, ("row", "depth", "col"))
    cells = cells.reshape(n_row, n_depth, n_col, held, CW_DEV)
    block = min(held, rows, 1024)
    row_base = row_id * tile_rows + core * rows
    col_base = col_id * tile_cols
    col_first = col_base // block
    left, deg_left, tile = panel(
        cells, row_base // block, col_first, rows, tile_cols, block, genes, True
    )
    right, deg_right = panel(
        cells, col_first, col_first, tile_cols, tile_cols, block, genes, False
    )
    k_rows = jnp.sum(deg_left, axis=1, keepdims=True)
    k_cols = jnp.sum(deg_right, axis=1)[None, :]
    pieces = 4
    size = rows // pieces
    swap = [(i, i ^ 1) for i in range(n_depth)]
    whole = None
    arrived = []
    for index in range(pieces):
        piece, whole = margin_piece(
            left, right, tile, k_rows, k_cols, index, pieces, core, col_base - row_base, whole
        )
        arrived.append(lax.ppermute(piece, "depth", swap))
    for index in range(pieces):
        start = (1 - core) * rows + index * size
        whole = lax.dynamic_update_slice_in_dim(whole, arrived[index], start, 0)
    return whole


def solution(mesh):
    return jax.shard_map(
        on_device,
        mesh=mesh,
        in_specs=(P("depth", "col"), P("depth")),
        out_specs=P("row", "col"),
        check_vma=False,
    )
```
